32 devices in a mesh: clips: 2 (over y), seq: 8 (over z, x), tp: 2 (over core).
Axes of the slice: x: 2, y: 2, z: 4, core: 2. Of those that a mesh axis runs over, the one named last changes fastest.
Arguments:
- video_q: bfloat16 [1024, 2048], P(('clips', 'seq'), 'tp'), parts along dimension 0, may hold values from -30 to 30
- video_k: bfloat16 [1024, 2048], P(('clips', 'seq'), 'tp'), parts along dimension 0, may hold values from -10 to 10
- video_v: bfloat16 [1024, 2048], P(('clips', 'seq'), 'tp'), parts along dimension 0, may hold values from -3 to 3
- audio_q: bfloat16 [256, 1024], P(('clips', 'seq'), 'tp'), parts along dimension 0, may hold values from -30 to 30
- audio_k: bfloat16 [256, 1024], P(('clips', 'seq'), 'tp'), parts along dimension 0, may hold values from -10 to 10
- audio_v: bfloat16 [256, 1024], P(('clips', 'seq'), 'tp'), parts along dimension 0, may hold values from -3 to 3
- video_cross_q: bfloat16 [1024, 1024], P(('clips', 'seq'), 'tp'), parts along dimension 0, may hold values from -40 to 40
- audio_cross_q: bfloat16 [256, 2048], P(('clips', 'seq'), 'tp'), parts along dimension 0, may hold values from -40 to 40
- audio_key_gain: float32 [64], replicated, may hold values from 0.5 to 2
- video_key_gain: float32 [128], replicated, may hold values from 0.5 to 2
Outputs:
- video_self: bfloat16 [1024, 2048], P(('clips', 'seq'), 'tp'), parts along dimension 0
- audio_self: bfloat16 [256, 1024], P(('clips', 'seq'), 'tp'), parts along dimension 0
- video_cross: bfloat16 [1024, 1024], P(('clips', 'seq'), 'tp'), parts along dimension 0
- audio_cross: bfloat16 [256, 2048], P(('clips', 'seq'), 'tp'), parts along dimension 0
The draws below stay inside these ranges and needn't reach their ends.
There are 2 independent parts, one for each index of `clips`. The reference program is written for one: setup_inputs(seed, part) draws one part's arguments, and reference() takes and returns one part's arrays. A program takes and returns all parts, laid end to end along the dimension named above; an argument that names none is the same for every part. Nothing has to cross between parts.
All inputs are finite; a program needn't handle non-finite values.
Results may differ from the reference program's by a relative error of at most 0.011.
Values may be sent and summed in bfloat16 or wider, within the bound.
A program may use at most 128 MiB of HBM per device.

```python
import math
import jax
import jax.numpy as jnp
from jax import lax

HEADS = 16
VHEAD = 128
AHEAD = 64
VTOKENS = 512
ATOKENS = 128


def base_rows(key, row_count, col_count, salt_value):
    subkey = jax.random.fold_in(key, salt_value)
    return jnp.clip(1.7 * jax.random.normal(subkey, (row_count, col_count), jnp.float32), -10.0, 10.0)


def drawn_queries(key, row_count, col_count, salt_value):
    own_rows = base_rows(key, row_count, col_count, salt_value + 1)
    return own_rows


def loud_queries(key, row_count, col_count, salt_value):
    own_rows = base_rows(key, row_count, col_count, salt_value)
    return own_rows


def draw_video_k(key, part):
    return base_rows(key, VTOKENS, HEADS * VHEAD, 101).astype(jnp.bfloat16)


def draw_video_q(key, part):
    return drawn_queries(key, VTOKENS, HEADS * VHEAD, 101).astype(jnp.bfloat16)


def draw_audio_k(key, part):
    return base_rows(key, ATOKENS, HEADS * AHEAD, 201).astype(jnp.bfloat16)


def draw_audio_q(key, part):
    return drawn_queries(key, ATOKENS, HEADS * AHEAD, 201).astype(jnp.bfloat16)


def draw_video_cross_q(key, part):
    return loud_queries(key, VTOKENS, HEADS * AHEAD, 301).astype(jnp.bfloat16)


def draw_audio_cross_q(key, part):
    return loud_queries(key, ATOKENS, HEADS * VHEAD, 401).astype(jnp.bfloat16)


def levels(key, extent, cuts, smallest, top_value):
    def one(dim, shards_of):
        draws = jax.random.uniform(jax.random.fold_in(jax.random.fold_in(key, 6), dim), (shards_of,), jnp.float32, smallest / len(cuts), top_value / len(cuts))
        return jnp.repeat(jnp.exp(draws), extent[dim] // shards_of).reshape((-1,) + (1,) * (len(extent) - dim - 1))

    factor_of = one(*cuts[0])
    for cut in cuts[1:]:
        factor_of = factor_of * one(*cut)
    return factor_of


def gaussian(key, shape, spread, bound, split=(), kind=jnp.bfloat16):
    drawn = spread * jax.random.normal(key, shape, jnp.float32)
    if split:
        drawn = drawn * levels(key, shape, split, -0.22, 0.18)
    return jnp.clip(drawn, -bound, bound).astype(kind)


def setup_inputs(seed: int = 0, part: int = 0) -> dict:
    seeds = jax.random.split(jax.random.key(seed), 11)
    part_splits = jax.random.split(jax.random.fold_in(seeds[10], part), 11)
    video_q = draw_video_q(jax.random.fold_in(jax.random.fold_in(seeds[10], part), 71), part)
    video_k = draw_video_k(jax.random.fold_in(jax.random.fold_in(seeds[10], part), 71), part)
    video_v = gaussian(part_splits[2], (VTOKENS, HEADS * VHEAD), 0.3, 3.0, ((0, 8), (1, 2)))
    audio_q = draw_audio_q(jax.random.fold_in(jax.random.fold_in(seeds[10], part), 71), part)
    audio_k = draw_audio_k(jax.random.fold_in(jax.random.fold_in(seeds[10], part), 71), part)
    audio_v = gaussian(part_splits[5], (ATOKENS, HEADS * AHEAD), 0.3, 3.0, ((0, 8), (1, 2)))
    video_cross_q = draw_video_cross_q(jax.random.fold_in(jax.random.fold_in(seeds[10], part), 71), part)
    audio_cross_q = draw_audio_cross_q(jax.random.fold_in(jax.random.fold_in(seeds[10], part), 71), part)
    audio_key_gain = jnp.clip(jnp.exp(jax.random.uniform(seeds[8], (AHEAD,), jnp.float32, math.log(0.5), math.log(2.0))), 0.5, 2.0)
    video_key_gain = jnp.clip(jnp.exp(jax.random.uniform(seeds[9], (VHEAD,), jnp.float32, math.log(0.5), math.log(2.0))), 0.5, 2.0)
    return dict(video_q=video_q, video_k=video_k, video_v=video_v, audio_q=audio_q, audio_k=audio_k, audio_v=audio_v, video_cross_q=video_cross_q, audio_cross_q=audio_cross_q, audio_key_gain=audio_key_gain, video_key_gain=video_key_gain)


def split_heads(matrix, head_size):
    return matrix.reshape(matrix.shape[0], matrix.shape[1] // head_size, head_size)

def attend(queries, key_rows, value_rows, head_size):
    q_heads = jnp.transpose(split_heads(queries, head_size), (1, 0, 2))
    k_heads = jnp.transpose(split_heads(key_rows, head_size), (1, 0, 2))
    v_heads = jnp.transpose(split_heads(value_rows, head_size), (1, 0, 2))

    def one_head(triple):
        q_one, k_one, v_one = triple
        scores = jnp.dot(q_one, k_one.T, preferred_element_type=jnp.float32) * (1.0 / math.sqrt(head_size))
        raised = jnp.exp(scores - lax.optimization_barrier(jnp.max(scores, axis=1, keepdims=True)))
        weighted = jnp.dot(raised.astype(jnp.bfloat16), v_one, preferred_element_type=jnp.float32)
        return weighted / lax.optimization_barrier(jnp.sum(raised, axis=1, keepdims=True))
    output = lax.map(one_head, (q_heads, k_heads, v_heads))
    return jnp.transpose(output, (1, 0, 2)).reshape(queries.shape[0], -1).astype(jnp.bfloat16)

def cross_keys(states, gain_vector, head_size):
    values = split_heads(states, head_size).astype(jnp.float32)
    factor = lax.rsqrt(lax.optimization_barrier(jnp.mean(values * values, axis=2, keepdims=True)) + 1e-06)
    return (values * factor * gain_vector).astype(jnp.bfloat16).reshape(states.shape)

def reference(video_q, video_k, video_v, audio_q, audio_k, audio_v, video_cross_q, audio_cross_q, audio_key_gain, video_key_gain):
    video_self = attend(video_q, video_k, video_v, VHEAD)
    audio_self = attend(audio_q, audio_k, audio_v, AHEAD)
    video_cross = attend(video_cross_q, cross_keys(audio_self, audio_key_gain, AHEAD), audio_self, AHEAD)
    audio_cross = attend(audio_cross_q, cross_keys(video_self, video_key_gain, VHEAD), video_self, VHEAD)
    return (video_self, audio_self, video_cross, audio_cross)
```

```python
import functools
import math

import jax
import jax.numpy as jnp
from jax import lax
from jax.experimental import pallas as pl
from jax.experimental.pallas import tpu as pltpu
from jax.sharding import PartitionSpec as P

VHEAD = 128
AHEAD = 64
LANES = 128
LOG2E = math.log2(math.e)


def split_heads(matrix, head_size):
    return matrix.reshape(matrix.shape[0], matrix.shape[1] // head_size, head_size)


def attend(queries, key_rows, value_rows, head_size):
    scores = jnp.einsum(
        "qhd,khd->hqk",
        split_heads(queries, head_size),
        split_heads(key_rows, head_size),
        preferred_element_type=jnp.float32,
    ) * (1.0 / math.sqrt(head_size))
    weights = jnp.exp(scores - jnp.max(scores, axis=2, keepdims=True))
    totals = jnp.sum(weights, axis=2)
    summed = jnp.einsum(
        "hqk,khd->hqd",
        weights.astype(jnp.bfloat16),
        split_heads(value_rows, head_size),
        preferred_element_type=jnp.float32,
    )
    output = summed / totals[:, :, None]
    return jnp.transpose(output, (1, 0, 2)).reshape(output.shape[1], -1).astype(jnp.bfloat16)


def cross_keys(states, gain_vector, head_size):
    values = split_heads(states, head_size).astype(jnp.float32)
    factor = lax.rsqrt(jnp.mean(values * values, axis=2, keepdims=True) + 1e-06)
    return (values * factor * gain_vector).astype(jnp.bfloat16).reshape(states.shape)


def gathered_shards(
    video_q, video_k, video_v, audio_q, audio_k, audio_v,
    video_cross_q, audio_cross_q, audio_key_gain, video_key_gain,
):
    def whole(x):
        return lax.all_gather(x, "seq", axis=0, tiled=True)

    audio_self = attend(audio_q, whole(audio_k), whole(audio_v), AHEAD)
    audio_whole = whole(audio_self)
    video_cross = attend(
        video_cross_q, cross_keys(audio_whole, audio_key_gain, AHEAD), audio_whole, AHEAD
    )
    video_self = attend(video_q, whole(video_k), whole(video_v), VHEAD)
    video_whole = whole(video_self)
    audio_cross = attend(
        audio_cross_q, cross_keys(video_whole, video_key_gain, VHEAD), video_whole, VHEAD
    )
    return (video_self, audio_self, video_cross, audio_cross)


def dot_t(a, b):
    return lax.dot_general(a, b, (((1,), (1,)), ((), ())), preferred_element_type=jnp.float32)


def soft(scores, head_size):
    top = jnp.max(scores, axis=1, keepdims=True)
    e = jnp.exp2((scores - top) * (LOG2E / math.sqrt(head_size)))
    return e.astype(jnp.bfloat16), 1.0 / jnp.sum(e, axis=1, keepdims=True)


def one_head(q, k, v):
    w, inv = soft(dot_t(q, k), VHEAD)
    return (jnp.dot(w, v, preferred_element_type=jnp.float32) * inv).astype(jnp.bfloat16)


def head_pair(q, k, v, low):
    zero = jnp.zeros_like(q)
    lowq = low[: q.shape[0]]
    wa, ia = soft(dot_t(jnp.where(lowq, q, zero), k), AHEAD)
    wb, ib = soft(dot_t(jnp.where(lowq, zero, q), k), AHEAD)
    oa = jnp.dot(wa, v, preferred_element_type=jnp.float32) * ia
    ob = jnp.dot(wb, v, preferred_element_type=jnp.float32) * ib
    return jnp.where(lowq, oa, ob).astype(jnp.bfloat16)


def kernel(
    n, vt, at,
    vq, vk, vv, aq, ak, av, vcq, acq, again, vgain,
    o_vs, o_as, o_vc, o_ac,
    vstage, astage, cstage, vrecv, arecv, crecv, vs_buf, as_buf, vc_buf, ac_buf,
    stage_sem, send_sem, recv_sem,
):
    me = lax.axis_index("seq")
    half = n // 2
    my_half = me // half
    my_pair = lax.rem(me, half)
    kv_rows, v_rows = 2 * vt, 3 * vt + at
    KV, QA, AU, CQ, OVS, OAS, OVC, OAC = range(8)

    stages = [
        (vk, vstage.at[pl.ds(0, vt)]),
        (vv, vstage.at[pl.ds(vt, vt)]),
        (vq, vstage.at[pl.ds(2 * vt, vt)]),
        (acq, vstage.at[pl.ds(3 * vt, at)]),
        (aq, astage.at[pl.ds(0, at)]),
        (ak, astage.at[pl.ds(at, at)]),
        (av, astage.at[pl.ds(2 * at, at)]),
        (vcq, cstage),
    ]
    stages = [pltpu.make_async_copy(s, d, stage_sem.at[i]) for i, (s, d) in enumerate(stages)]
    for c in stages:
        c.start()

    barrier = pltpu.get_barrier_semaphore()
    for k in range(1, n):
        pl.semaphore_signal(
            barrier, inc=1, device_id={"seq": lax.rem(me + k, n)},
            device_id_type=pl.DeviceIdType.MESH,
        )
    for c in stages:
        c.wait()
    pl.semaphore_wait(barrier, n - 1)

    order = sorted(range(1, n), key=lambda k: abs(k - half))
    near = list(range(1, half))

    def lanes(ref, rows, block):
        return ref.at[rows, pl.ds(pl.multiple_of(block * LANES, LANES), LANES)]

    def remote(src, dst, kind, peer):
        pltpu.make_async_remote_copy(
            src_ref=src, dst_ref=dst, send_sem=send_sem.at[kind], recv_sem=recv_sem.at[kind],
            device_id={"seq": peer}, device_id_type=pl.DeviceIdType.MESH,
        ).start()

    def local(src, dst, kind):
        pltpu.make_async_copy(src, dst, recv_sem.at[kind]).start()

    def drain(ref, sem):
        pltpu.make_async_copy(ref, ref, sem).wait()

    everyone = [lax.rem(me + k, n) for k in order]
    halfmates = [my_half * half + lax.rem(my_pair + k, half) for k in near]

    kv, qa = pl.ds(0, kv_rows), pl.ds(kv_rows, v_rows - kv_rows)
    for rows, kind in ((kv, KV), (qa, QA)):
        for peer in everyone:
            remote(lanes(vstage, rows, peer), vrecv.at[me, rows], kind, peer)
        local(lanes(vstage, rows, me), vrecv.at[me, rows], kind)
    for peer in everyone:
        remote(lanes(astage, slice(None), lax.rem(peer, half)), arecv.at[me], AU, peer)
    local(lanes(astage, slice(None), my_pair), arecv.at[me], AU)
    for peer in halfmates:
        remote(lanes(cstage, slice(None), lax.rem(peer, half)), crecv.at[my_pair], CQ, peer)
    local(lanes(cstage, slice(None), my_pair), crecv.at[my_pair], CQ)

    drain(vrecv.at[:, kv], recv_sem.at[KV])
    drain(vrecv.at[:, qa], recv_sem.at[QA])
    key_rows = vrecv[:, :vt].reshape(n * vt, VHEAD)
    value_rows = vrecv[:, vt : 2 * vt].reshape(n * vt, VHEAD)
    for i in range(0, n, 2):
        q = vrecv[i : i + 2, 2 * vt : 3 * vt].reshape(2 * vt, VHEAD)
        vs_buf[i : i + 2] = one_head(q, key_rows, value_rows).reshape(2, vt, VHEAD)
    for peer in everyone:
        remote(vs_buf.at[peer], lanes(o_vs, slice(None), me), OVS, peer)
    local(vs_buf.at[me], lanes(o_vs, slice(None), me), OVS)

    states = vs_buf[...].reshape(n * vt, VHEAD)
    x = states.astype(jnp.float32)
    factor = lax.rsqrt(jnp.sum(x * x, axis=1, keepdims=True) * (1.0 / VHEAD) + 1e-06)
    normed = (x * factor * vgain[...]).astype(jnp.bfloat16)
    q = vrecv[:, 3 * vt :].reshape(n * at, VHEAD)
    ac_buf[...] = one_head(q, normed, states).reshape(n, at, VHEAD)
    for peer in everyone:
        remote(ac_buf.at[peer], lanes(o_ac, slice(None), me), OAC, peer)
    local(ac_buf.at[me], lanes(o_ac, slice(None), me), OAC)

    drain(arecv, recv_sem.at[AU])
    low = lax.broadcasted_iota(jnp.int32, (half * vt, LANES), 1) < AHEAD
    states = head_pair(
        arecv[:, :at].reshape(n * at, LANES),
        arecv[:, at : 2 * at].reshape(n * at, LANES),
        arecv[:, 2 * at :].reshape(n * at, LANES),
        low,
    )
    as_buf[...] = states.reshape(n, at, LANES)
    for peer in halfmates:
        remote(as_buf.at[peer], lanes(o_as, slice(None), my_pair), OAS, peer)
    local(as_buf.at[me], lanes(o_as, slice(None), my_pair), OAS)

    x = states.astype(jnp.float32)
    lowx = low[: n * at]
    square = x * x
    zero = jnp.zeros_like(square)
    means = jnp.where(
        lowx,
        jnp.sum(jnp.where(lowx, square, zero), axis=1, keepdims=True),
        jnp.sum(jnp.where(lowx, zero, square), axis=1, keepdims=True),
    ) * (1.0 / AHEAD)
    gain = jnp.concatenate([again[...], again[...]], axis=1)
    normed = (x * lax.rsqrt(means + 1e-06) * gain).astype(jnp.bfloat16)
    drain(crecv, recv_sem.at[CQ])
    q = crecv[...].reshape(half * vt, LANES)
    vc_buf[...] = head_pair(q, normed, states, low).reshape(half, vt, LANES)
    for peer in halfmates:
        remote(vc_buf.at[lax.rem(peer, half)], lanes(o_vc, slice(None), my_pair), OVC, peer)
    local(vc_buf.at[my_pair], lanes(o_vc, slice(None), my_pair), OVC)

    far, mates = pl.ds(0, n - 1), pl.ds(0, half - 1)
    drain(vrecv.at[far, kv], send_sem.at[KV])
    drain(vrecv.at[far, qa], send_sem.at[QA])
    drain(arecv.at[far], send_sem.at[AU])
    drain(crecv.at[mates], send_sem.at[CQ])
    drain(vs_buf.at[far], send_sem.at[OVS])
    drain(ac_buf.at[far], send_sem.at[OAC])
    drain(as_buf.at[mates], send_sem.at[OAS])
    drain(vc_buf.at[mates], send_sem.at[OVC])
    drain(o_vs, recv_sem.at[OVS])
    drain(o_as, recv_sem.at[OAS])
    drain(o_vc, recv_sem.at[OVC])
    drain(o_ac, recv_sem.at[OAC])


def exchanged_shards(
    n, video_q, video_k, video_v, audio_q, audio_k, audio_v,
    video_cross_q, audio_cross_q, audio_key_gain, video_key_gain,
):
    vt, at = video_q.shape[0], audio_q.shape[0]
    half = n // 2
    bf = jnp.bfloat16
    anywhere = pl.BlockSpec(memory_space=pl.ANY)
    vmem = pl.BlockSpec(memory_space=pltpu.VMEM)
    outs = [video_q, audio_q, video_cross_q, audio_cross_q]
    return pl.pallas_call(
        functools.partial(kernel, n, vt, at),
        out_shape=[jax.ShapeDtypeStruct(x.shape, bf) for x in outs],
        in_specs=[anywhere] * 8 + [vmem] * 2,
        out_specs=[anywhere] * 4,
        scratch_shapes=[
            pltpu.VMEM((3 * vt + at, video_q.shape[1]), bf),
            pltpu.VMEM((3 * at, audio_q.shape[1]), bf),
            pltpu.VMEM((vt, video_cross_q.shape[1]), bf),
            pltpu.VMEM((n, 3 * vt + at, LANES), bf),
            pltpu.VMEM((n, 3 * at, LANES), bf),
            pltpu.VMEM((half, vt, LANES), bf),
            pltpu.VMEM((n, vt, LANES), bf),
            pltpu.VMEM((n, at, LANES), bf),
            pltpu.VMEM((half, vt, LANES), bf),
            pltpu.VMEM((n, at, LANES), bf),
            pltpu.SemaphoreType.DMA((8,)),
            pltpu.SemaphoreType.DMA((8,)),
            pltpu.SemaphoreType.DMA((8,)),
        ],
        compiler_params=pltpu.CompilerParams(
            collective_id=0, has_side_effects=True, vmem_limit_bytes=32 * 2**20
        ),
    )(
        video_q, video_k, video_v, audio_q, audio_k, audio_v, video_cross_q, audio_cross_q,
        audio_key_gain.reshape(1, AHEAD), video_key_gain.reshape(1, VHEAD),
    )


def solution(mesh):
    n = mesh.shape["seq"]

    def shards(*args):
        video_heads = args[0].shape[1] // VHEAD
        audio_pairs = args[3].shape[1] // (2 * AHEAD)
        if video_heads == n and 2 * audio_pairs == n:
            return tuple(exchanged_shards(n, *args))
        return gathered_shards(*args)

    split = P(("clips", "seq"), "tp")
    return jax.shard_map(
        shards,
        mesh=mesh,
        in_specs=(split,) * 8 + (P(), P()),
        out_specs=(split,) * 4,
        check_vma=False,
    )
```

```python
import functools
import math

import jax
import jax.numpy as jnp
from jax import lax
from jax.experimental import pallas as pl
from jax.experimental.pallas import tpu as pltpu
from jax.sharding import PartitionSpec as P

VHEAD = 128
AHEAD = 64
LANES = 128
LOG2E = math.log2(math.e)


def split_heads(matrix, head_size):
    return matrix.reshape(matrix.shape[0], matrix.shape[1] // head_size, head_size)


def attend(queries, key_rows, value_rows, head_size):
    scores = jnp.einsum(
        "qhd,khd->hqk",
        split_heads(queries, head_size),
        split_heads(key_rows, head_size),
        preferred_element_type=jnp.float32,
    ) * (1.0 / math.sqrt(head_size))
    weights = jnp.exp(scores - jnp.max(scores, axis=2, keepdims=True))
    totals = jnp.sum(weights, axis=2)
    summed = jnp.einsum(
        "hqk,khd->hqd",
        weights.astype(jnp.bfloat16),
        split_heads(value_rows, head_size),
        preferred_element_type=jnp.float32,
    )
    output = summed / totals[:, :, None]
    return jnp.transpose(output, (1, 0, 2)).reshape(output.shape[1], -1).astype(jnp.bfloat16)


def cross_keys(states, gain_vector, head_size):
    values = split_heads(states, head_size).astype(jnp.float32)
    factor = lax.rsqrt(jnp.mean(values * values, axis=2, keepdims=True) + 1e-06)
    return (values * factor * gain_vector).astype(jnp.bfloat16).reshape(states.shape)


def gathered_shards(
    video_q, video_k, video_v, audio_q, audio_k, audio_v,
    video_cross_q, audio_cross_q, audio_key_gain, video_key_gain,
):
    def whole(x):
        return lax.all_gather(x, "seq", axis=0, tiled=True)

    audio_self = attend(audio_q, whole(audio_k), whole(audio_v), AHEAD)
    audio_whole = whole(audio_self)
    video_cross = attend(
        video_cross_q, cross_keys(audio_whole, audio_key_gain, AHEAD), audio_whole, AHEAD
    )
    video_self = attend(video_q, whole(video_k), whole(video_v), VHEAD)
    video_whole = whole(video_self)
    audio_cross = attend(
        audio_cross_q, cross_keys(video_whole, video_key_gain, VHEAD), video_whole, VHEAD
    )
    return (video_self, audio_self, video_cross, audio_cross)


def dot_t(a, b):
    return lax.dot_general(a, b, (((1,), (1,)), ((), ())), preferred_element_type=jnp.float32)


def soft(scores, head_size):
    top = jnp.max(scores, axis=1, keepdims=True)
    e = jnp.exp2((scores - top) * (LOG2E / math.sqrt(head_size)))
    return e.astype(jnp.bfloat16), 1.0 / jnp.sum(e, axis=1, keepdims=True)


def one_head(q, k, v):
    w, inv = soft(dot_t(q, k), VHEAD)
    return (jnp.dot(w, v, preferred_element_type=jnp.float32) * inv).astype(jnp.bfloat16)


def head_pair(q, k, v, low):
    zero = jnp.zeros_like(q)
    lowq = low[: q.shape[0]]
    wa, ia = soft(dot_t(jnp.where(lowq, q, zero), k), AHEAD)
    wb, ib = soft(dot_t(jnp.where(lowq, zero, q), k), AHEAD)
    oa = jnp.dot(wa, v, preferred_element_type=jnp.float32) * ia
    ob = jnp.dot(wb, v, preferred_element_type=jnp.float32) * ib
    return jnp.where(lowq, oa, ob).astype(jnp.bfloat16)


def kernel(
    n, vt, at,
    vq, vk, vv, aq, ak, av, vcq, acq, again, vgain,
    o_vs, o_as, o_vc, o_ac,
    vstage, astage, cstage, vrecv, arecv, crecv, vs_buf, as_buf, vc_buf, ac_buf,
    stage_sem, send_sem, recv_sem,
):
    me = lax.axis_index("seq")
    half = n // 2
    my_half = me // half
    my_pair = lax.rem(me, half)
    kv_rows, v_rows = 2 * vt, 3 * vt + at
    KV, QA, AU, CQ, OVS, OAS, OVC, OAC = range(8)

    stages = [
        (vk, vstage.at[pl.ds(0, vt)]),
        (vv, vstage.at[pl.ds(vt, vt)]),
        (vq, vstage.at[pl.ds(2 * vt, vt)]),
        (acq, vstage.at[pl.ds(3 * vt, at)]),
        (aq, astage.at[pl.ds(0, at)]),
        (ak, astage.at[pl.ds(at, at)]),
        (av, astage.at[pl.ds(2 * at, at)]),
        (vcq, cstage),
    ]
    stages = [pltpu.make_async_copy(s, d, stage_sem.at[i]) for i, (s, d) in enumerate(stages)]
    for c in stages:
        c.start()

    barrier = pltpu.get_barrier_semaphore()
    for k in range(1, n):
        pl.semaphore_signal(
            barrier, inc=1, device_id={"seq": lax.rem(me + k, n)},
            device_id_type=pl.DeviceIdType.MESH,
        )
    for c in stages:
        c.wait()
    pl.semaphore_wait(barrier, n - 1)

    def lanes(ref, rows, block):
        return ref.at[rows, pl.ds(pl.multiple_of(block * LANES, LANES), LANES)]

    def remote(src, dst, kind, peer):
        pltpu.make_async_remote_copy(
            src_ref=src, dst_ref=dst, send_sem=send_sem.at[kind], recv_sem=recv_sem.at[kind],
            device_id={"seq": peer}, device_id_type=pl.DeviceIdType.MESH,
        ).start()

    def local(src, dst, kind):
        pltpu.make_async_copy(src, dst, recv_sem.at[kind]).start()

    def drain(ref, sem):
        pltpu.make_async_copy(ref, ref, sem).wait()

    other = (1 - my_half) * half
    far_peers = [other + lax.rem(my_pair + k, half) for k in range(half)]
    near_peers = [my_half * half + lax.rem(my_pair + k, half) for k in range(1, half)]
    everyone = far_peers + near_peers

    kv, qa = pl.ds(0, kv_rows), pl.ds(kv_rows, v_rows - kv_rows)
    for peers in (far_peers, near_peers):
        for rows, kind in ((kv, KV), (qa, QA)):
            for peer in peers:
                remote(lanes(vstage, rows, peer), vrecv.at[me, rows], kind, peer)
    for rows, kind in ((kv, KV), (qa, QA)):
        local(lanes(vstage, rows, me), vrecv.at[me, rows], kind)
    for peer in everyone:
        remote(lanes(astage, slice(None), lax.rem(peer, half)), arecv.at[me], AU, peer)
    local(lanes(astage, slice(None), my_pair), arecv.at[me], AU)
    for peer in near_peers:
        remote(lanes(cstage, slice(None), lax.rem(peer, half)), crecv.at[my_pair], CQ, peer)
    local(lanes(cstage, slice(None), my_pair), crecv.at[my_pair], CQ)

    drain(vrecv.at[:, kv], recv_sem.at[KV])
    drain(vrecv.at[:, qa], recv_sem.at[QA])
    key_rows = vrecv[:, :vt].reshape(n * vt, VHEAD)
    value_rows = vrecv[:, vt : 2 * vt].reshape(n * vt, VHEAD)
    for i in range(0, n, 2):
        q = vrecv[i : i + 2, 2 * vt : 3 * vt].reshape(2 * vt, VHEAD)
        vs_buf[i : i + 2] = one_head(q, key_rows, value_rows).reshape(2, vt, VHEAD)
    for peer in everyone:
        remote(vs_buf.at[peer], lanes(o_vs, slice(None), me), OVS, peer)
    local(vs_buf.at[me], lanes(o_vs, slice(None), me), OVS)

    states = vs_buf[...].reshape(n * vt, VHEAD)
    x = states.astype(jnp.float32)
    factor = lax.rsqrt(jnp.sum(x * x, axis=1, keepdims=True) * (1.0 / VHEAD) + 1e-06)
    normed = (x * factor * vgain[...]).astype(jnp.bfloat16)
    q = vrecv[:, 3 * vt :].reshape(n * at, VHEAD)
    ac_buf[...] = one_head(q, normed, states).reshape(n, at, VHEAD)
    for peer in everyone:
        remote(ac_buf.at[peer], lanes(o_ac, slice(None), me), OAC, peer)
    local(ac_buf.at[me], lanes(o_ac, slice(None), me), OAC)

    drain(arecv, recv_sem.at[AU])
    low = lax.broadcasted_iota(jnp.int32, (half * vt, LANES), 1) < AHEAD
    states = head_pair(
        arecv[:, :at].reshape(n * at, LANES),
        arecv[:, at : 2 * at].reshape(n * at, LANES),
        arecv[:, 2 * at :].reshape(n * at, LANES),
        low,
    )
    as_buf[...] = states.reshape(n, at, LANES)
    for peer in near_peers:
        remote(as_buf.at[peer], lanes(o_as, slice(None), my_pair), OAS, peer)
    local(as_buf.at[me], lanes(o_as, slice(None), my_pair), OAS)

    x = states.astype(jnp.float32)
    lowx = low[: n * at]
    square = x * x
    zero = jnp.zeros_like(square)
    means = jnp.where(
        lowx,
        jnp.sum(jnp.where(lowx, square, zero), axis=1, keepdims=True),
        jnp.sum(jnp.where(lowx, zero, square), axis=1, keepdims=True),
    ) * (1.0 / AHEAD)
    gain = jnp.concatenate([again[...], again[...]], axis=1)
    normed = (x * lax.rsqrt(means + 1e-06) * gain).astype(jnp.bfloat16)
    drain(crecv, recv_sem.at[CQ])
    q = crecv[...].reshape(half * vt, LANES)
    vc_buf[...] = head_pair(q, normed, states, low).reshape(half, vt, LANES)
    for peer in near_peers:
        remote(vc_buf.at[lax.rem(peer, half)], lanes(o_vc, slice(None), my_pair), OVC, peer)
    local(vc_buf.at[my_pair], lanes(o_vc, slice(None), my_pair), OVC)

    far, mates = pl.ds(0, n - 1), pl.ds(0, half - 1)
    drain(vrecv.at[far, kv], send_sem.at[KV])
    drain(vrecv.at[far, qa], send_sem.at[QA])
    drain(arecv.at[far], send_sem.at[AU])
    drain(crecv.at[mates], send_sem.at[CQ])
    drain(vs_buf.at[far], send_sem.at[OVS])
    drain(ac_buf.at[far], send_sem.at[OAC])
    drain(as_buf.at[mates], send_sem.at[OAS])
    drain(vc_buf.at[mates], send_sem.at[OVC])
    drain(o_vs, recv_sem.at[OVS])
    drain(o_as, recv_sem.at[OAS])
    drain(o_vc, recv_sem.at[OVC])
    drain(o_ac, recv_sem.at[OAC])


def hand_over(*refs):
    sems = refs[8]
    copies = [pltpu.make_async_copy(refs[i], refs[4 + i], sems.at[i]) for i in range(4)]
    for c in copies:
        c.start()
    for c in copies:
        c.wait()


def exchanged_shards(
    n, video_q, video_k, video_v, audio_q, audio_k, audio_v,
    video_cross_q, audio_cross_q, audio_key_gain, video_key_gain,
):
    vt, at = video_q.shape[0], audio_q.shape[0]
    half = n // 2
    bf = jnp.bfloat16
    anywhere = pl.BlockSpec(memory_space=pl.ANY)
    vmem = pl.BlockSpec(memory_space=pltpu.VMEM)
    outs = [video_q, audio_q, video_cross_q, audio_cross_q]
    results = pl.pallas_call(
        functools.partial(kernel, n, vt, at),
        out_shape=[pltpu.VMEM(x.shape, bf) for x in outs],
        in_specs=[anywhere] * 8 + [vmem] * 2,
        out_specs=[vmem] * 4,
        scratch_shapes=[
            pltpu.VMEM((3 * vt + at, video_q.shape[1]), bf),
            pltpu.VMEM((3 * at, audio_q.shape[1]), bf),
            pltpu.VMEM((vt, video_cross_q.shape[1]), bf),
            pltpu.VMEM((n, 3 * vt + at, LANES), bf),
            pltpu.VMEM((n, 3 * at, LANES), bf),
            pltpu.VMEM((half, vt, LANES), bf),
            pltpu.VMEM((n, vt, LANES), bf),
            pltpu.VMEM((n, at, LANES), bf),
            pltpu.VMEM((half, vt, LANES), bf),
            pltpu.VMEM((n, at, LANES), bf),
            pltpu.SemaphoreType.DMA((8,)),
            pltpu.SemaphoreType.DMA((8,)),
            pltpu.SemaphoreType.DMA((8,)),
        ],
        compiler_params=pltpu.CompilerParams(
            collective_id=0, has_side_effects=True, vmem_limit_bytes=60 * 2**20
        ),
    )(
        video_q, video_k, video_v, audio_q, audio_k, audio_v, video_cross_q, audio_cross_q,
        audio_key_gain.reshape(1, AHEAD), video_key_gain.reshape(1, VHEAD),
    )
    return pl.pallas_call(
        hand_over,
        out_shape=[jax.ShapeDtypeStruct(x.shape, bf) for x in outs],
        in_specs=[vmem] * 4,
        out_specs=[anywhere] * 4,
        scratch_shapes=[pltpu.SemaphoreType.DMA((4,))],
    )(*[pltpu.with_memory_space_constraint(r, pltpu.VMEM) for r in results])


def solution(mesh):
    n = mesh.shape["seq"]

    def shards(*args):
        video_heads = args[0].shape[1] // VHEAD
        audio_pairs = args[3].shape[1] // (2 * AHEAD)
        if video_heads == n and 2 * audio_pairs == n:
            return tuple(exchanged_shards(n, *args))
        return gathered_shards(*args)

    split = P(("clips", "seq"), "tp")
    return jax.shard_map(
        shards,
        mesh=mesh,
        in_specs=(split,) * 8 + (P(), P()),
        out_specs=(split,) * 4,
        check_vma=False,
    )
```

```python
import functools
import math

import jax
import jax.numpy as jnp
from jax import lax
from jax.experimental import pallas as pl
from jax.experimental.pallas import tpu as pltpu
from jax.sharding import PartitionSpec as P

VHEAD = 128
AHEAD = 64
LANES = 128
LOG2E = math.log2(math.e)


def split_heads(matrix, head_size):
    return matrix.reshape(matrix.shape[0], matrix.shape[1] // head_size, head_size)


def attend(queries, key_rows, value_rows, head_size):
    scores = jnp.einsum(
        "qhd,khd->hqk",
        split_heads(queries, head_size),
        split_heads(key_rows, head_size),
        preferred_element_type=jnp.float32,
    ) * (1.0 / math.sqrt(head_size))
    weights = jnp.exp(scores - jnp.max(scores, axis=2, keepdims=True))
    totals = jnp.sum(weights, axis=2)
    summed = jnp.einsum(
        "hqk,khd->hqd",
        weights.astype(jnp.bfloat16),
        split_heads(value_rows, head_size),
        preferred_element_type=jnp.float32,
    )
    output = summed / totals[:, :, None]
    return jnp.transpose(output, (1, 0, 2)).reshape(output.shape[1], -1).astype(jnp.bfloat16)


def cross_keys(states, gain_vector, head_size):
    values = split_heads(states, head_size).astype(jnp.float32)
    factor = lax.rsqrt(jnp.mean(values * values, axis=2, keepdims=True) + 1e-06)
    return (values * factor * gain_vector).astype(jnp.bfloat16).reshape(states.shape)


def gathered_shards(
    video_q, video_k, video_v, audio_q, audio_k, audio_v,
    video_cross_q, audio_cross_q, audio_key_gain, video_key_gain,
):
    def whole(x):
        return lax.all_gather(x, "seq", axis=0, tiled=True)

    audio_self = attend(audio_q, whole(audio_k), whole(audio_v), AHEAD)
    audio_whole = whole(audio_self)
    video_cross = attend(
        video_cross_q, cross_keys(audio_whole, audio_key_gain, AHEAD), audio_whole, AHEAD
    )
    video_self = attend(video_q, whole(video_k), whole(video_v), VHEAD)
    video_whole = whole(video_self)
    audio_cross = attend(
        audio_cross_q, cross_keys(video_whole, video_key_gain, VHEAD), video_whole, VHEAD
    )
    return (video_self, audio_self, video_cross, audio_cross)


def dot_t(a, b):
    return lax.dot_general(a, b, (((1,), (1,)), ((), ())), preferred_element_type=jnp.float32)


def soft(scores, head_size):
    top = jnp.max(scores, axis=1, keepdims=True)
    e = jnp.exp2((scores - top) * (LOG2E / math.sqrt(head_size)))
    return e.astype(jnp.bfloat16), 1.0 / jnp.sum(e, axis=1, keepdims=True)


def one_head(q, k, v):
    w, inv = soft(dot_t(q, k), VHEAD)
    return (jnp.dot(w, v, preferred_element_type=jnp.float32) * inv).astype(jnp.bfloat16)


def head_pair(q, k, v, low):
    zero = jnp.zeros_like(q)
    lowq = low[: q.shape[0]]
    wa, ia = soft(dot_t(jnp.where(lowq, q, zero), k), AHEAD)
    wb, ib = soft(dot_t(jnp.where(lowq, zero, q), k), AHEAD)
    oa = jnp.dot(wa, v, preferred_element_type=jnp.float32) * ia
    ob = jnp.dot(wb, v, preferred_element_type=jnp.float32) * ib
    return jnp.where(lowq, oa, ob).astype(jnp.bfloat16)


def kernel(
    n, vt, at,
    vq, vk, vv, aq, ak, av, vcq, acq, again, vgain,
    o_vs, o_as, o_vc, o_ac,
    vstage, astage, cstage, vrecv, arecv, crecv, vs_buf, as_buf, vc_buf, ac_buf, key_buf,
    stage_sem, send_sem, recv_sem, query_sem,
):
    me = lax.axis_index("seq")
    half = n // 2
    my_half = me // half
    my_pair = lax.rem(me, half)
    kv_rows, v_rows = 2 * vt, 3 * vt + at
    KV, QA, AU, CQ, OVS, OAS, OVC, OAC = range(8)

    stages = [
        (vk, vstage.at[pl.ds(0, vt)]),
        (vv, vstage.at[pl.ds(vt, vt)]),
        (vq, vstage.at[pl.ds(2 * vt, vt)]),
        (acq, vstage.at[pl.ds(3 * vt, at)]),
        (aq, astage.at[pl.ds(0, at)]),
        (ak, astage.at[pl.ds(at, at)]),
        (av, astage.at[pl.ds(2 * at, at)]),
        (vcq, cstage),
    ]
    stages = [pltpu.make_async_copy(s, d, stage_sem.at[i]) for i, (s, d) in enumerate(stages)]
    barrier = pltpu.get_barrier_semaphore()
    for k in range(1, n):
        pl.semaphore_signal(
            barrier, inc=1, device_id={"seq": lax.rem(me + k, n)},
            device_id_type=pl.DeviceIdType.MESH,
        )
    for c in stages:
        c.start()
    for c in stages[:2]:
        c.wait()
    pl.semaphore_wait(barrier, n - 1)

    def lanes(ref, rows, block):
        return ref.at[rows, pl.ds(pl.multiple_of(block * LANES, LANES), LANES)]

    def remote(src, dst, kind, peer):
        pltpu.make_async_remote_copy(
            src_ref=src, dst_ref=dst, send_sem=send_sem.at[kind], recv_sem=recv_sem.at[kind],
            device_id={"seq": peer}, device_id_type=pl.DeviceIdType.MESH,
        ).start()

    def local(src, dst, kind):
        pltpu.make_async_copy(src, dst, recv_sem.at[kind]).start()

    def drain(ref, sem):
        pltpu.make_async_copy(ref, ref, sem).wait()

    other = (1 - my_half) * half
    far_peers = [other + lax.rem(my_pair + k, half) for k in range(half)]
    near_peers = [my_half * half + lax.rem(my_pair + k, half) for k in range(1, half)]
    everyone = far_peers + near_peers

    kv, qa = pl.ds(0, kv_rows), pl.ds(kv_rows, v_rows - kv_rows)
    for peer in everyone:
        remote(lanes(vstage, kv, peer), vrecv.at[me, kv], KV, peer)
    local(lanes(vstage, kv, me), vrecv.at[me, kv], KV)
    for c in stages[2:]:
        c.wait()
    pltpu.make_async_copy(lanes(vstage, qa, me), vrecv.at[me, qa], query_sem.at[me]).start()
    for peer in everyone:
        pltpu.make_async_remote_copy(
            src_ref=lanes(vstage, qa, peer), dst_ref=vrecv.at[me, qa],
            send_sem=send_sem.at[QA], recv_sem=query_sem.at[me],
            device_id={"seq": peer}, device_id_type=pl.DeviceIdType.MESH,
        ).start()
    for peer in everyone:
        remote(lanes(astage, slice(None), lax.rem(peer, half)), arecv.at[me], AU, peer)
    local(lanes(astage, slice(None), my_pair), arecv.at[me], AU)
    for peer in near_peers:
        remote(lanes(cstage, slice(None), lax.rem(peer, half)), crecv.at[my_pair], CQ, peer)
    local(lanes(cstage, slice(None), my_pair), crecv.at[my_pair], CQ)

    drain(vrecv.at[:, kv], recv_sem.at[KV])
    key_rows = vrecv[:, :vt].reshape(n * vt, VHEAD)
    value_rows = vrecv[:, vt : 2 * vt].reshape(n * vt, VHEAD)
    arrivals = [base + lax.rem(my_pair - k + half, half) for base in (my_half * half, other) for k in range(half)]
    own = arrivals[0]
    for first, second in zip(arrivals[::2], arrivals[1::2]):
        pair = (first, second)
        for source in pair:
            drain(vrecv.at[source, qa], query_sem.at[source])
        q = jnp.concatenate([vrecv[source, 2 * vt : 3 * vt] for source in pair], axis=0)
        states = one_head(q, key_rows, value_rows)
        for source, rows in zip(pair, (states[:vt], states[vt:])):
            vs_buf[source] = rows
        x = states.astype(jnp.float32)
        factor = lax.rsqrt(jnp.sum(x * x, axis=1, keepdims=True) * (1.0 / VHEAD) + 1e-06)
        normed = (x * factor * vgain[...]).astype(jnp.bfloat16)
        for source, rows in zip(pair, (normed[:vt], normed[vt:])):
            key_buf[source] = rows
        for source in pair:
            if source is own:
                local(vs_buf.at[me], lanes(o_vs, slice(None), me), OVS)
            else:
                remote(vs_buf.at[source], lanes(o_vs, slice(None), me), OVS, source)

    q = vrecv[:, 3 * vt :].reshape(n * at, VHEAD)
    keys, states = key_buf[...].reshape(n * vt, VHEAD), vs_buf[...].reshape(n * vt, VHEAD)
    ac_buf[...] = one_head(q, keys, states).reshape(n, at, VHEAD)
    for peer in everyone:
        remote(ac_buf.at[peer], lanes(o_ac, slice(None), me), OAC, peer)
    local(ac_buf.at[me], lanes(o_ac, slice(None), me), OAC)

    drain(arecv, recv_sem.at[AU])
    low = lax.broadcasted_iota(jnp.int32, (half * vt, LANES), 1) < AHEAD
    states = head_pair(
        arecv[:, :at].reshape(n * at, LANES),
        arecv[:, at : 2 * at].reshape(n * at, LANES),
        arecv[:, 2 * at :].reshape(n * at, LANES),
        low,
    )
    as_buf[...] = states.reshape(n, at, LANES)
    for peer in near_peers:
        remote(as_buf.at[peer], lanes(o_as, slice(None), my_pair), OAS, peer)
    local(as_buf.at[me], lanes(o_as, slice(None), my_pair), OAS)

    x = states.astype(jnp.float32)
    lowx = low[: n * at]
    square = x * x
    zero = jnp.zeros_like(square)
    means = jnp.where(
        lowx,
        jnp.sum(jnp.where(lowx, square, zero), axis=1, keepdims=True),
        jnp.sum(jnp.where(lowx, zero, square), axis=1, keepdims=True),
    ) * (1.0 / AHEAD)
    gain = jnp.concatenate([again[...], again[...]], axis=1)
    normed = (x * lax.rsqrt(means + 1e-06) * gain).astype(jnp.bfloat16)
    drain(crecv, recv_sem.at[CQ])
    q = crecv[...].reshape(half * vt, LANES)
    vc_buf[...] = head_pair(q, normed, states, low).reshape(half, vt, LANES)
    for peer in near_peers:
        remote(vc_buf.at[lax.rem(peer, half)], lanes(o_vc, slice(None), my_pair), OVC, peer)
    local(vc_buf.at[my_pair], lanes(o_vc, slice(None), my_pair), OVC)

    far, mates = pl.ds(0, n - 1), pl.ds(0, half - 1)
    drain(vrecv.at[far, kv], send_sem.at[KV])
    drain(vrecv.at[far, qa], send_sem.at[QA])
    drain(arecv.at[far], send_sem.at[AU])
    drain(crecv.at[mates], send_sem.at[CQ])
    drain(vs_buf.at[far], send_sem.at[OVS])
    drain(ac_buf.at[far], send_sem.at[OAC])
    drain(as_buf.at[mates], send_sem.at[OAS])
    drain(vc_buf.at[mates], send_sem.at[OVC])
    drain(o_vs, recv_sem.at[OVS])
    drain(o_as, recv_sem.at[OAS])
    drain(o_vc, recv_sem.at[OVC])
    drain(o_ac, recv_sem.at[OAC])


def hand_over(*refs):
    sems = refs[8]
    copies = [pltpu.make_async_copy(refs[i], refs[4 + i], sems.at[i]) for i in range(4)]
    for c in copies:
        c.start()
    for c in copies:
        c.wait()


def exchanged_shards(
    n, video_q, video_k, video_v, audio_q, audio_k, audio_v,
    video_cross_q, audio_cross_q, audio_key_gain, video_key_gain,
):
    vt, at = video_q.shape[0], audio_q.shape[0]
    half = n // 2
    bf = jnp.bfloat16
    anywhere = pl.BlockSpec(memory_space=pl.ANY)
    vmem = pl.BlockSpec(memory_space=pltpu.VMEM)
    outs = [video_q, audio_q, video_cross_q, audio_cross_q]
    results = pl.pallas_call(
        functools.partial(kernel, n, vt, at),
        out_shape=[pltpu.VMEM(x.shape, bf) for x in outs],
        in_specs=[anywhere] * 8 + [vmem] * 2,
        out_specs=[vmem] * 4,
        scratch_shapes=[
            pltpu.VMEM((3 * vt + at, video_q.shape[1]), bf),
            pltpu.VMEM((3 * at, audio_q.shape[1]), bf),
            pltpu.VMEM((vt, video_cross_q.shape[1]), bf),
            pltpu.VMEM((n, 3 * vt + at, LANES), bf),
            pltpu.VMEM((n, 3 * at, LANES), bf),
            pltpu.VMEM((half, vt, LANES), bf),
            pltpu.VMEM((n, vt, LANES), bf),
            pltpu.VMEM((n, at, LANES), bf),
            pltpu.VMEM((half, vt, LANES), bf),
            pltpu.VMEM((n, at, LANES), bf),
            pltpu.VMEM((n, vt, LANES), bf),
            pltpu.SemaphoreType.DMA((8,)),
            pltpu.SemaphoreType.DMA((8,)),
            pltpu.SemaphoreType.DMA((8,)),
            pltpu.SemaphoreType.DMA((n,)),
        ],
        compiler_params=pltpu.CompilerParams(
            collective_id=0, has_side_effects=True, vmem_limit_bytes=60 * 2**20
        ),
    )(
        video_q, video_k, video_v, audio_q, audio_k, audio_v, video_cross_q, audio_cross_q,
        audio_key_gain.reshape(1, AHEAD), video_key_gain.reshape(1, VHEAD),
    )
    return pl.pallas_call(
        hand_over,
        out_shape=[jax.ShapeDtypeStruct(x.shape, bf) for x in outs],
        in_specs=[vmem] * 4,
        out_specs=[anywhere] * 4,
        scratch_shapes=[pltpu.SemaphoreType.DMA((4,))],
    )(*[pltpu.with_memory_space_constraint(r, pltpu.VMEM) for r in results])


def solution(mesh):
    n = mesh.shape["seq"]

    def shards(*args):
        video_heads = args[0].shape[1] // VHEAD
        audio_pairs = args[3].shape[1] // (2 * AHEAD)
        if video_heads == n and 2 * audio_pairs == n:
            return tuple(exchanged_shards(n, *args))
        return gathered_shards(*args)

    split = P(("clips", "seq"), "tp")
    return jax.shard_map(
        shards,
        mesh=mesh,
        in_specs=(split,) * 8 + (P(), P()),
        out_specs=(split,) * 4,
        check_vma=False,
    )
```
